32 devices in a mesh: grp: 2 (over y), row: 4 (over z), col: 4 (over x, core).
Axes of the slice: x: 2, y: 2, z: 4, core: 2. Of those that a mesh axis runs over, the one named last changes fastest.
Arguments:
- activations: bfloat16 [64, 6144], P(('grp', 'row'), 'col'), parts along dimension 0, may hold values from -6 to 6
- up_weight: bfloat16 [6144, 49152], P('col', 'row'), may hold values from -0.078125 to 0.078125
- up_bias: float32 [49152], P('row'), may hold values from -3 to 3
- cotangent: bfloat16 [64, 49152], P(('grp', 'col'), 'row'), parts along dimension 0, may hold values from -6 to 6
Outputs:
- hidden: bfloat16 [64, 49152], P(('grp', 'col'), 'row'), parts along dimension 0
- act_grad: bfloat16 [64, 6144], P(('grp', 'row'), 'col'), parts along dimension 0
- weight_grad: bfloat16 [12288, 49152], P(('grp', 'col'), 'row'), parts along dimension 0
- bias_grad: float32 [98304], P(('grp', 'row')), parts along dimension 0
The draws below stay inside these ranges and needn't reach their ends.
There are 2 independent parts, one for each index of `grp`. The reference program is written for one: setup_inputs(seed, part) draws one part's arguments, and reference() takes and returns one part's arrays. A program takes and returns all parts, laid end to end along the dimension named above; an argument that names none is the same for every part. Nothing has to cross between parts.
All inputs are finite; a program needn't handle non-finite values.
Results may differ from the reference program's by a relative error of at most 0.0049.
Values may be sent and summed in bfloat16 or wider, within the bound.
A program may use at most 256 MiB of HBM per device.

```python
import jax
import jax.numpy as jnp
from jax import lax

D = 6144
FF = 49152
TOKENS = 32


def with_spikes(drawn, rng, source, target, blocks, factor):
    owner, partner = [(jnp.arange(drawn.shape[axis_at]) // (drawn.shape[axis_at] // blocks)).reshape([-1 if axis == axis_at else 1 for axis in range(drawn.ndim)]) for axis_at in (source, target)]
    chosen = jax.random.permutation(rng, blocks)[partner]
    strong = (owner == chosen) | (owner == (partner + blocks // 2) % blocks)
    return jnp.where(strong, factor * drawn, drawn)


def levels(stream_key, extent, cuts, smallest, top_value):
    factor_of = 1.0
    for axis_at, parts in cuts:
        draws = jax.random.uniform(jax.random.fold_in(jax.random.fold_in(stream_key, 6), axis_at), (parts,), jnp.float32, smallest / len(cuts), top_value / len(cuts))
        factor_of = factor_of * jnp.repeat(jnp.exp(draws), extent[axis_at] // parts).reshape((-1,) + (1,) * (len(extent) - 1 - axis_at))
    return factor_of


def noise(key, shape, deviation, reach, shards=(), kind=jnp.bfloat16):
    factor_of = levels(key, shape, shards, -0.22, 0.18) if shards else 1.0
    result = jax.random.normal(key, shape, jnp.float32) * deviation * factor_of
    return jnp.minimum(jnp.maximum(result, -reach), reach).astype(kind)


def noise_with(rng, shape, width, reach, split, heavy, kind=jnp.bfloat16):
    values = width * jax.random.normal(rng, shape, jnp.float32)
    if split:
        values = values * levels(rng, shape, split, -0.22, 0.18)
    return jnp.clip(with_spikes(values, jax.random.fold_in(rng, 3), *heavy), -reach, reach).astype(kind)


def setup_inputs(seed: int = 0, part: int = 0) -> dict:
    arg_keys = jax.random.split(jax.random.key(seed), 5)
    own_keys = jax.random.split(jax.random.fold_in(arg_keys[4], part), 5)
    return {
        "activations": noise(own_keys[0], (TOKENS, D), 1.0, 6.0, ((0, 4), (1, 4))),
        "up_weight": noise(arg_keys[1], (D, FF), D ** -0.5, 0.078125, ((0, 4), (1, 4))),
        "up_bias": noise(arg_keys[2], (FF,), 0.5, 3.0, ((0, 4),), jnp.float32),
        "cotangent": noise_with(own_keys[3], (TOKENS, FF), 1.0, 6.0, ((0, 4), (1, 4)), (1, 0, 4, 2.0)),
    }


root_coef = 0.7978845608028654
cube_coef = 0.044715


def gelu_tanh(value):
    inner = root_coef * (value + cube_coef * value * value * value)
    return 0.5 * value * (1.0 + jnp.tanh(inner))


def gelu_slope(value):
    inner = root_coef * (value + cube_coef * value * value * value)
    tanh_val = jnp.tanh(inner)
    return 0.5 * (1.0 + tanh_val) + 0.5 * value * (1.0 - tanh_val * tanh_val) * root_coef * (1.0 + 3.0 * cube_coef * value * value)


def reference(activations, up_weight, up_bias, cotangent):
    pre = jnp.dot(activations, up_weight, preferred_element_type=jnp.float32) + up_bias.astype(jnp.float32)
    hidden = gelu_tanh(pre).astype(jnp.bfloat16)
    grad_pre = (cotangent.astype(jnp.float32) * gelu_slope(pre)).astype(jnp.bfloat16)
    act_grad = lax.dot_general(grad_pre, up_weight, (((1,), (1,)), ((), ())), preferred_element_type=jnp.float32).astype(jnp.bfloat16)
    weight_grad = lax.dot_general(activations, grad_pre, (((0,), (0,)), ((), ())), preferred_element_type=jnp.float32).astype(jnp.bfloat16)
    bias_grad = jnp.sum(grad_pre.astype(jnp.float32), axis=0)
    return hidden, act_grad, weight_grad, bias_grad
```

```python
import functools

import jax
import jax.numpy as jnp
from jax import lax
from jax.experimental import pallas as pl
from jax.experimental.pallas import tpu as pltpu
from jax.sharding import PartitionSpec as P

root_coef = 0.7978845608028654
cube_coef = 0.044715
MESH = pl.DeviceIdType.MESH
F32 = jnp.float32
BF16 = jnp.bfloat16


def gelu_tanh(value):
    inner = root_coef * (value + cube_coef * value * value * value)
    return 0.5 * value * (1.0 + jnp.tanh(inner))


def gelu_slope(value):
    inner = root_coef * (value + cube_coef * value * value * value)
    tanh_val = jnp.tanh(inner)
    return 0.5 * (1.0 + tanh_val) + 0.5 * value * (1.0 - tanh_val * tanh_val) * root_coef * (
        1.0 + 3.0 * cube_coef * value * value
    )


def general_per_device(activations, up_weight, up_bias, cotangent):
    gathered = lax.all_gather(activations, "row", axis=0, tiled=True)
    partial_value = jnp.dot(gathered, up_weight, preferred_element_type=jnp.float32)
    pre = lax.psum_scatter(partial_value, "col", scatter_dimension=0, tiled=True) + up_bias
    hidden = gelu_tanh(pre).astype(jnp.bfloat16)
    grad_own = (cotangent.astype(jnp.float32) * gelu_slope(pre)).astype(jnp.bfloat16)
    grad_pre = lax.all_gather(grad_own, "col", axis=0, tiled=True)
    bias_grad = jnp.sum(grad_pre.astype(jnp.float32), axis=0)
    weight_sum = lax.dot_general(
        gathered, grad_pre, (((0,), (0,)), ((), ())), preferred_element_type=jnp.float32
    )
    weight_grad = weight_sum.astype(jnp.bfloat16)
    act_grad = lax.psum_scatter(
        lax.dot_general(
            grad_pre, up_weight, (((1,), (1,)), ((), ())), preferred_element_type=jnp.float32
        ),
        "row",
        scatter_dimension=0,
        tiled=True,
    ).astype(jnp.bfloat16)
    return (hidden, act_grad, weight_grad, bias_grad)


def exchange_kernel(
    chunks, act, weight, bias, cot,
    hidden_out, act_grad_out, x_out, grad_out,
    wbuf, ag, x32, cbuf, bbuf, part, r1, s2, r2, gbuf, g32, hbuf, acc, r3, obuf,
    w_sem, in_sem, ag_send, ag_recv, s1_send, s1_recv, s2_send, s2_recv,
    gp_send, gp_recv, gx_send, gx_recv, gf_send, gf_recv, r3_send, r3_recv, out_sem, gout_sem,
):
    rows = ag.shape[0]
    width = wbuf.shape[2]
    feats = wbuf.shape[1]
    row = lax.axis_index("row")
    col = lax.axis_index("col")
    x = lax.div(col, 2)
    core = lax.rem(col, 2)
    mate = 2 * x + (1 - core)
    across = 2 * (1 - x) + core
    diag = 2 * (1 - x) + (1 - core)

    def w_copy(k):
        return pltpu.make_async_copy(
            weight.at[:, pl.ds(pl.multiple_of(k * width, 128), width)], wbuf.at[k], w_sem.at[k]
        )

    own_copy = pltpu.make_async_copy(act, ag.at[row], in_sem.at[0])
    own_copy.start()
    w_copy(0).start()
    cot_copy = pltpu.make_async_copy(cot, cbuf, in_sem.at[1])
    bias_copy = pltpu.make_async_copy(bias, bbuf, in_sem.at[2])

    barrier = pltpu.get_barrier_semaphore()
    for d in range(1, rows):
        pl.semaphore_signal(
            barrier, inc=1, device_id={"row": lax.rem(row + d, rows)}, device_id_type=MESH
        )
    for peer in (mate, across):
        pl.semaphore_signal(barrier, inc=1, device_id={"col": peer}, device_id_type=MESH)
    pl.semaphore_wait(barrier, rows + 1)

    ag_copies = [
        pltpu.make_async_remote_copy(
            src_ref=act, dst_ref=ag.at[row], send_sem=ag_send.at[d - 1], recv_sem=ag_recv.at[d - 1],
            device_id={"row": lax.rem(row + d, rows)}, device_id_type=MESH,
        )
        for d in range(1, rows)
    ]
    for copy in ag_copies:
        copy.start()
    for k in range(1, chunks):
        w_copy(k).start()
    cot_copy.start()
    bias_copy.start()

    own_copy.wait()
    for copy in ag_copies:
        copy.wait_recv()
    x32[...] = jnp.concatenate([ag[i].astype(F32) for i in range(rows)], axis=0).astype(BF16)
    x_copy = pltpu.make_async_copy(x32, x_out, out_sem.at[0])
    x_copy.start()
    acc[...] = jnp.zeros_like(acc)
    cot_copy.wait()
    bias_copy.wait()

    def s1_copy(k):
        return pltpu.make_async_remote_copy(
            src_ref=part.at[k, 1 - core], dst_ref=r1.at[k], send_sem=s1_send.at[k],
            recv_sem=s1_recv.at[k], device_id={"col": mate}, device_id_type=MESH,
        )

    def s2_copy(k):
        return pltpu.make_async_remote_copy(
            src_ref=s2.at[k], dst_ref=r2.at[k], send_sem=s2_send.at[k],
            recv_sem=s2_recv.at[k], device_id={"col": across}, device_id_type=MESH,
        )

    def gp_copy(k):
        return pltpu.make_async_remote_copy(
            src_ref=gbuf.at[k, col], dst_ref=gbuf.at[k, col], send_sem=gp_send.at[k],
            recv_sem=gp_recv.at[k], device_id={"col": mate}, device_id_type=MESH,
        )

    def gx_copy(k):
        return pltpu.make_async_remote_copy(
            src_ref=gbuf.at[k, col], dst_ref=gbuf.at[k, col], send_sem=gx_send.at[k],
            recv_sem=gx_recv.at[k], device_id={"col": across}, device_id_type=MESH,
        )

    def gf_copy(k):
        return pltpu.make_async_remote_copy(
            src_ref=gbuf.at[k, across], dst_ref=gbuf.at[k, across], send_sem=gf_send.at[k],
            recv_sem=gf_recv.at[k], device_id={"col": mate}, device_id_type=MESH,
        )

    def g_out(k):
        return pltpu.make_async_copy(g32.at[k], grad_out.at[k], gout_sem.at[k])

    tile = 512 if width % 512 == 0 else 256
    ftile = 512 if feats % 512 == 0 else 256

    def dot_up(k):
        w_copy(k).wait()

        def body(i, carry):
            cols = pl.ds(pl.multiple_of(i * tile, tile), tile)
            out = jnp.dot(x32[...], wbuf[k, :, cols], preferred_element_type=F32)
            for j in range(4):
                part[k, j % 2, j // 2, :, cols] = out[8 * j : 8 * j + 8]
            return carry

        lax.fori_loop(0, width // tile, body, 0)
        s1_copy(k).start()

    def pair_sum(k):
        s1_copy(k).wait_recv()
        s2[k] = part[k, core, 1 - x] + r1[k, 1 - x]
        s2_copy(k).start()

    def activate(k):
        s2_copy(k).wait_recv()
        cols = pl.ds(pl.multiple_of(k * width, 128), width)
        pre = part[k, core, x] + r1[k, x] + r2[k] + bbuf[:, cols]
        hbuf[:, cols] = gelu_tanh(pre).astype(BF16)
        gbuf[k, col] = (cbuf[:, cols].astype(F32) * gelu_slope(pre)).astype(BF16)
        gx_copy(k).start()
        gp_copy(k).start()

    def forward(k):
        gx_copy(k).wait_recv()
        gf_copy(k).start()

    def dot_down(k):
        gp_copy(k).wait_recv()
        gf_copy(k).wait_recv()
        grad = jnp.concatenate([gbuf[k, i].astype(F32) for i in range(4)], axis=0).astype(BF16)
        g32[k] = grad
        g_out(k).start()

        def body(i, carry):
            feat = pl.ds(pl.multiple_of(i * ftile, ftile), ftile)
            acc[:, feat] += lax.dot_general(
                g32[k], wbuf[k, feat, :], (((1,), (1,)), ((), ())), preferred_element_type=F32
            )
            return carry

        lax.fori_loop(0, feats // ftile, body, 0)

    def stages(t, carry):
        for lag, stage in enumerate((dot_up, pair_sum, activate, forward, dot_down)):
            k = t - lag
            pl.when(jnp.logical_and(k >= 0, k < chunks))(functools.partial(stage, k))
        return carry

    lax.fori_loop(0, chunks + 4, stages, 0)

    hidden_copy = pltpu.make_async_copy(hbuf, hidden_out, out_sem.at[1])
    hidden_copy.start()
    r3_copies = []
    for d in range(1, rows):
        to = lax.rem(row + d, rows)
        copy = pltpu.make_async_remote_copy(
            src_ref=acc.at[pl.ds(pl.multiple_of(to * 8, 8), 8)], dst_ref=r3.at[d - 1],
            send_sem=r3_send.at[d - 1], recv_sem=r3_recv.at[d - 1],
            device_id={"row": to}, device_id_type=MESH,
        )
        copy.start()
        r3_copies.append(copy)

    def drain(k, carry):
        s1_copy(k).wait_send()
        s2_copy(k).wait_send()
        gp_copy(k).wait_send()
        gx_copy(k).wait_send()
        gf_copy(k).wait_send()
        g_out(k).wait()
        return carry

    lax.fori_loop(0, chunks, drain, 0)
    for copy in ag_copies:
        copy.wait_send()
    x_copy.wait()
    total = acc[pl.ds(pl.multiple_of(row * 8, 8), 8)]
    for d, copy in enumerate(r3_copies):
        copy.wait_recv()
        total += r3[d]
    obuf[...] = total.astype(BF16)
    act_copy = pltpu.make_async_copy(obuf, act_grad_out, out_sem.at[2])
    act_copy.start()
    for copy in r3_copies:
        copy.wait_send()
    hidden_copy.wait()
    act_copy.wait()


def outer_kernel(x_ref, grad_ref, hidden_in, act_in, w_ref, bias_ref, hidden_out, act_out, xt, sems):
    k, i = pl.program_id(0), pl.program_id(1)
    last = jnp.logical_and(k == pl.num_programs(0) - 1, i == pl.num_programs(1) - 1)
    copies = (
        pltpu.make_async_copy(hidden_in, hidden_out, sems.at[0]),
        pltpu.make_async_copy(act_in, act_out, sems.at[1]),
    )

    @pl.when(jnp.logical_and(k == 0, i == 0))
    def _():
        for copy in copies:
            copy.start()
        xt[...] = jnp.transpose(x_ref[...].astype(F32)).astype(BF16)

    @pl.when(i == 0)
    def _():
        bias_ref[...] = jnp.sum(grad_ref[0].astype(F32), axis=0, keepdims=True)

    height = w_ref.shape[0]
    step = 128

    def body(n, carry):
        at = pl.multiple_of(n * step, step)
        lhs = xt[pl.ds(pl.multiple_of(i * height + at, step), step), :]
        w_ref[pl.ds(at, step), :] = jnp.dot(
            lhs, grad_ref[0], preferred_element_type=F32
        ).astype(BF16)
        return carry

    lax.fori_loop(0, height // step, body, 0)

    @pl.when(last)
    def _():
        for copy in copies:
            copy.wait()


def fast_per_device(activations, up_weight, up_bias, cotangent, *, rows, chunks):
    feats, hidden_units = up_weight.shape
    width = hidden_units // chunks
    any_spec = pl.BlockSpec(memory_space=pl.ANY)
    dma = pltpu.SemaphoreType.DMA
    hidden, act_grad, x_all, grad_all = pl.pallas_call(
        functools.partial(exchange_kernel, chunks),
        out_shape=(
            jax.ShapeDtypeStruct((8, hidden_units), BF16),
            jax.ShapeDtypeStruct((8, feats), BF16),
            jax.ShapeDtypeStruct((32, feats), BF16),
            jax.ShapeDtypeStruct((chunks, 32, width), BF16),
        ),
        in_specs=[any_spec] * 4,
        out_specs=(any_spec,) * 4,
        scratch_shapes=[
            pltpu.VMEM((chunks, feats, width), BF16),
            pltpu.VMEM((rows, 8, feats), BF16),
            pltpu.VMEM((32, feats), BF16),
            pltpu.VMEM((8, hidden_units), BF16),
            pltpu.VMEM((1, hidden_units), F32),
            pltpu.VMEM((chunks, 2, 2, 8, width), F32),
            pltpu.VMEM((chunks, 2, 8, width), F32),
            pltpu.VMEM((chunks, 8, width), F32),
            pltpu.VMEM((chunks, 8, width), F32),
            pltpu.VMEM((chunks, 4, 8, width), BF16),
            pltpu.VMEM((chunks, 32, width), BF16),
            pltpu.VMEM((8, hidden_units), BF16),
            pltpu.VMEM((32, feats), F32),
            pltpu.VMEM((rows - 1, 8, feats), F32),
            pltpu.VMEM((8, feats), BF16),
            dma((chunks,)), dma((3,)), dma((rows - 1,)), dma((rows - 1,)),
            dma((chunks,)), dma((chunks,)), dma((chunks,)), dma((chunks,)),
            dma((chunks,)), dma((chunks,)), dma((chunks,)), dma((chunks,)),
            dma((chunks,)), dma((chunks,)), dma((rows - 1,)), dma((rows - 1,)),
            dma((3,)), dma((chunks,)),
        ],
        compiler_params=pltpu.CompilerParams(
            collective_id=0, has_side_effects=True, vmem_limit_bytes=56 * 1024 * 1024
        ),
    )(activations, up_weight, up_bias.reshape(1, hidden_units), cotangent)

    split = 2
    weight_grad, bias_grad, hidden, act_grad = pl.pallas_call(
        outer_kernel,
        grid=(chunks, split),
        out_shape=(
            jax.ShapeDtypeStruct((feats, hidden_units), BF16),
            jax.ShapeDtypeStruct((1, hidden_units), F32),
            jax.ShapeDtypeStruct((8, hidden_units), BF16),
            jax.ShapeDtypeStruct((8, feats), BF16),
        ),
        in_specs=[
            pl.BlockSpec((32, feats), lambda k, i: (0, 0)),
            pl.BlockSpec((1, 32, width), lambda k, i: (k, 0, 0)),
            any_spec,
            any_spec,
        ],
        out_specs=(
            pl.BlockSpec((feats // split, width), lambda k, i: (i, k)),
            pl.BlockSpec((1, width), lambda k, i: (0, k)),
            any_spec,
            any_spec,
        ),
        scratch_shapes=[pltpu.VMEM((feats, 32), BF16), dma((2,))],
        compiler_params=pltpu.CompilerParams(vmem_limit_bytes=40 * 1024 * 1024),
    )(x_all, grad_all, hidden, act_grad)
    return hidden, act_grad, weight_grad, bias_grad.reshape(hidden_units)


def solution(mesh):
    in_specs = (P(("grp", "row"), "col"), P("col", "row"), P("row"), P(("grp", "col"), "row"))
    out_specs = (
        P(("grp", "col"), "row"),
        P(("grp", "row"), "col"),
        P(("grp", "col"), "row"),
        P(("grp", "row")),
    )
    rows, cols = mesh.shape["row"], mesh.shape["col"]

    def per_device(activations, up_weight, up_bias, cotangent):
        feats, hidden_units = up_weight.shape
        chunks = 8
        fits = (
            rows == 4
            and cols == 4
            and activations.shape[0] == 8
            and cotangent.shape[0] == 8
            and feats % 256 == 0
            and hidden_units % (chunks * 256) == 0
            and feats * hidden_units <= 1536 * 12288
        )
        if fits:
            return fast_per_device(
                activations, up_weight, up_bias, cotangent, rows=rows, chunks=chunks
            )
        return general_per_device(activations, up_weight, up_bias, cotangent)

    return jax.shard_map(
        per_device, mesh=mesh, in_specs=in_specs, out_specs=out_specs, check_vma=False
    )
```

```python
import functools

import jax
import jax.numpy as jnp
from jax import lax
from jax.experimental import pallas as pl
from jax.experimental.pallas import tpu as pltpu
from jax.sharding import PartitionSpec as P

root_coef = 0.7978845608028654
cube_coef = 0.044715
MESH = pl.DeviceIdType.MESH
F32 = jnp.float32
BF16 = jnp.bfloat16


def gelu_tanh(value):
    inner = root_coef * (value + cube_coef * value * value * value)
    return 0.5 * value * (1.0 + jnp.tanh(inner))


def gelu_slope(value):
    inner = root_coef * (value + cube_coef * value * value * value)
    tanh_val = jnp.tanh(inner)
    return 0.5 * (1.0 + tanh_val) + 0.5 * value * (1.0 - tanh_val * tanh_val) * root_coef * (
        1.0 + 3.0 * cube_coef * value * value
    )


def general_per_device(activations, up_weight, up_bias, cotangent):
    gathered = lax.all_gather(activations, "row", axis=0, tiled=True)
    partial_value = jnp.dot(gathered, up_weight, preferred_element_type=jnp.float32)
    pre = lax.psum_scatter(partial_value, "col", scatter_dimension=0, tiled=True) + up_bias
    hidden = gelu_tanh(pre).astype(jnp.bfloat16)
    grad_own = (cotangent.astype(jnp.float32) * gelu_slope(pre)).astype(jnp.bfloat16)
    grad_pre = lax.all_gather(grad_own, "col", axis=0, tiled=True)
    bias_grad = jnp.sum(grad_pre.astype(jnp.float32), axis=0)
    weight_sum = lax.dot_general(
        gathered, grad_pre, (((0,), (0,)), ((), ())), preferred_element_type=jnp.float32
    )
    weight_grad = weight_sum.astype(jnp.bfloat16)
    act_grad = lax.psum_scatter(
        lax.dot_general(
            grad_pre, up_weight, (((1,), (1,)), ((), ())), preferred_element_type=jnp.float32
        ),
        "row",
        scatter_dimension=0,
        tiled=True,
    ).astype(jnp.bfloat16)
    return (hidden, act_grad, weight_grad, bias_grad)


def exchange_kernel(
    chunks, act, weight, bias, cot,
    hidden_out, act_grad_out, x_out, grad_out,
    wbuf, ag, x32, cbuf, bbuf, part, r1, s2, r2, gbuf, g32, hbuf, acc, r3, obuf,
    w_sem, in_sem, ag_send, ag_recv, s1_send, s1_recv, s2_send, s2_recv,
    gp_send, gp_recv, gx_send, gx_recv, gf_send, gf_recv, r3_send, r3_recv, out_sem, gout_sem,
):
    rows = ag.shape[0]
    width = wbuf.shape[2]
    feats = wbuf.shape[1]
    row = lax.axis_index("row")
    col = lax.axis_index("col")
    x = lax.div(col, 2)
    core = lax.rem(col, 2)
    mate = 2 * x + (1 - core)
    across = 2 * (1 - x) + core
    diag = 2 * (1 - x) + (1 - core)

    def w_copy(k):
        return pltpu.make_async_copy(
            weight.at[:, pl.ds(pl.multiple_of(k * width, 128), width)], wbuf.at[k], w_sem.at[k]
        )

    own_copy = pltpu.make_async_copy(act, ag.at[row], in_sem.at[0])
    own_copy.start()
    w_copy(0).start()
    cot_copy = pltpu.make_async_copy(cot, cbuf, in_sem.at[1])
    bias_copy = pltpu.make_async_copy(bias, bbuf, in_sem.at[2])

    barrier = pltpu.get_barrier_semaphore()
    for d in range(1, rows):
        pl.semaphore_signal(
            barrier, inc=1, device_id={"row": lax.rem(row + d, rows)}, device_id_type=MESH
        )
    for peer in (mate, across):
        pl.semaphore_signal(barrier, inc=1, device_id={"col": peer}, device_id_type=MESH)
    pl.semaphore_wait(barrier, rows + 1)

    ag_copies = [
        pltpu.make_async_remote_copy(
            src_ref=act, dst_ref=ag.at[row], send_sem=ag_send.at[d - 1], recv_sem=ag_recv.at[d - 1],
            device_id={"row": lax.rem(row + d, rows)}, device_id_type=MESH,
        )
        for d in range(1, rows)
    ]
    for copy in ag_copies:
        copy.start()
    for k in range(1, chunks):
        w_copy(k).start()
    cot_copy.start()
    bias_copy.start()

    own_copy.wait()
    for copy in ag_copies:
        copy.wait_recv()
    x32[...] = jnp.concatenate([ag[i].astype(F32) for i in range(rows)], axis=0).astype(BF16)
    x_copy = pltpu.make_async_copy(x32, x_out, out_sem.at[0])
    x_copy.start()
    acc[...] = jnp.zeros_like(acc)
    cot_copy.wait()
    bias_copy.wait()

    def s1_copy(k):
        return pltpu.make_async_remote_copy(
            src_ref=part.at[k, 1 - core], dst_ref=r1.at[k], send_sem=s1_send.at[k],
            recv_sem=s1_recv.at[k], device_id={"col": mate}, device_id_type=MESH,
        )

    def s2_copy(k):
        return pltpu.make_async_remote_copy(
            src_ref=s2.at[k], dst_ref=r2.at[k], send_sem=s2_send.at[k],
            recv_sem=s2_recv.at[k], device_id={"col": across}, device_id_type=MESH,
        )

    def gp_copy(k):
        return pltpu.make_async_remote_copy(
            src_ref=gbuf.at[k, col], dst_ref=gbuf.at[k, col], send_sem=gp_send.at[k],
            recv_sem=gp_recv.at[k], device_id={"col": mate}, device_id_type=MESH,
        )

    def gx_copy(k):
        return pltpu.make_async_remote_copy(
            src_ref=gbuf.at[k, col], dst_ref=gbuf.at[k, col], send_sem=gx_send.at[k],
            recv_sem=gx_recv.at[k], device_id={"col": across}, device_id_type=MESH,
        )

    def gf_copy(k):
        return pltpu.make_async_remote_copy(
            src_ref=gbuf.at[k, across], dst_ref=gbuf.at[k, across], send_sem=gf_send.at[k],
            recv_sem=gf_recv.at[k], device_id={"col": mate}, device_id_type=MESH,
        )

    def g_out(k):
        return pltpu.make_async_copy(g32.at[k], grad_out.at[k], gout_sem.at[k])

    def dot_up(k):
        w_copy(k).wait()

        out = jnp.dot(x32[...], wbuf[k], preferred_element_type=F32)
        for j in range(4):
            part[k, j % 2, j // 2] = out[8 * j : 8 * j + 8]
        s1_copy(k).start()

    def pair_sum(k):
        s1_copy(k).wait_recv()
        s2[k] = (part[k, core, 1 - x] + r1[k, 1 - x]).astype(BF16)
        s2_copy(k).start()

    def activate(k):
        s2_copy(k).wait_recv()
        cols = pl.ds(pl.multiple_of(k * width, 128), width)
        pre = part[k, core, x] + r1[k, x] + r2[k].astype(F32) + bbuf[:, cols]
        hbuf[:, cols] = gelu_tanh(pre).astype(BF16)
        gbuf[k, col] = (cbuf[:, cols].astype(F32) * gelu_slope(pre)).astype(BF16)
        gx_copy(k).start()
        gp_copy(k).start()

    def forward(k):
        gx_copy(k).wait_recv()
        gf_copy(k).start()

    def dot_down(k):
        gp_copy(k).wait_recv()
        gf_copy(k).wait_recv()
        grad = jnp.concatenate([gbuf[k, i].astype(F32) for i in range(4)], axis=0).astype(BF16)
        g32[k] = grad
        g_out(k).start()

        acc[...] += lax.dot_general(
            grad, wbuf[k], (((1,), (1,)), ((), ())), preferred_element_type=F32
        )

    def stages(t, carry):
        for lag, stage in ((0, dot_up), (2, pair_sum), (4, activate), (6, forward), (8, dot_down)):
            k = t - lag
            pl.when(jnp.logical_and(k >= 0, k < chunks))(functools.partial(stage, k))
        return carry

    lax.fori_loop(0, chunks + 8, stages, 0)

    hidden_copy = pltpu.make_async_copy(hbuf, hidden_out, out_sem.at[1])
    hidden_copy.start()
    r3_copies = []
    for d in range(1, rows):
        to = lax.rem(row + d, rows)
        copy = pltpu.make_async_remote_copy(
            src_ref=acc.at[pl.ds(pl.multiple_of(to * 8, 8), 8)], dst_ref=r3.at[d - 1],
            send_sem=r3_send.at[d - 1], recv_sem=r3_recv.at[d - 1],
            device_id={"row": to}, device_id_type=MESH,
        )
        copy.start()
        r3_copies.append(copy)

    def drain(k, carry):
        s1_copy(k).wait_send()
        s2_copy(k).wait_send()
        gp_copy(k).wait_send()
        gx_copy(k).wait_send()
        gf_copy(k).wait_send()
        g_out(k).wait()
        return carry

    lax.fori_loop(0, chunks, drain, 0)
    for copy in ag_copies:
        copy.wait_send()
    x_copy.wait()
    total = acc[pl.ds(pl.multiple_of(row * 8, 8), 8)]
    for d, copy in enumerate(r3_copies):
        copy.wait_recv()
        total += r3[d]
    obuf[...] = total.astype(BF16)
    act_copy = pltpu.make_async_copy(obuf, act_grad_out, out_sem.at[2])
    act_copy.start()
    for copy in r3_copies:
        copy.wait_send()
    hidden_copy.wait()
    act_copy.wait()


def outer_kernel(x_ref, grad_ref, hidden_in, act_in, w_ref, bias_ref, hidden_out, act_out, xt, sems):
    k, i = pl.program_id(0), pl.program_id(1)
    last = jnp.logical_and(k == pl.num_programs(0) - 1, i == pl.num_programs(1) - 1)
    copies = (
        pltpu.make_async_copy(hidden_in, hidden_out, sems.at[0]),
        pltpu.make_async_copy(act_in, act_out, sems.at[1]),
    )

    @pl.when(jnp.logical_and(k == 0, i == 0))
    def _():
        for copy in copies:
            copy.start()
        xt[...] = jnp.transpose(x_ref[...].astype(F32)).astype(BF16)

    @pl.when(i == 0)
    def _():
        bias_ref[...] = jnp.sum(grad_ref[0].astype(F32), axis=0, keepdims=True)

    height = w_ref.shape[0]
    lhs = xt[pl.ds(pl.multiple_of(i * height, height), height), :]
    w_ref[...] = jnp.dot(lhs, grad_ref[0], preferred_element_type=F32).astype(BF16)

    @pl.when(last)
    def _():
        for copy in copies:
            copy.wait()


def fast_per_device(activations, up_weight, up_bias, cotangent, *, rows, chunks):
    feats, hidden_units = up_weight.shape
    width = hidden_units // chunks
    any_spec = pl.BlockSpec(memory_space=pl.ANY)
    dma = pltpu.SemaphoreType.DMA
    hidden, act_grad, x_all, grad_all = pl.pallas_call(
        functools.partial(exchange_kernel, chunks),
        out_shape=(
            jax.ShapeDtypeStruct((8, hidden_units), BF16),
            jax.ShapeDtypeStruct((8, feats), BF16),
            jax.ShapeDtypeStruct((32, feats), BF16),
            jax.ShapeDtypeStruct((chunks, 32, width), BF16),
        ),
        in_specs=[any_spec] * 4,
        out_specs=(any_spec,) * 4,
        scratch_shapes=[
            pltpu.VMEM((chunks, feats, width), BF16),
            pltpu.VMEM((rows, 8, feats), BF16),
            pltpu.VMEM((32, feats), BF16),
            pltpu.VMEM((8, hidden_units), BF16),
            pltpu.VMEM((1, hidden_units), F32),
            pltpu.VMEM((chunks, 2, 2, 8, width), F32),
            pltpu.VMEM((chunks, 2, 8, width), F32),
            pltpu.VMEM((chunks, 8, width), BF16),
            pltpu.VMEM((chunks, 8, width), BF16),
            pltpu.VMEM((chunks, 4, 8, width), BF16),
            pltpu.VMEM((chunks, 32, width), BF16),
            pltpu.VMEM((8, hidden_units), BF16),
            pltpu.VMEM((32, feats), F32),
            pltpu.VMEM((rows - 1, 8, feats), F32),
            pltpu.VMEM((8, feats), BF16),
            dma((chunks,)), dma((3,)), dma((rows - 1,)), dma((rows - 1,)),
            dma((chunks,)), dma((chunks,)), dma((chunks,)), dma((chunks,)),
            dma((chunks,)), dma((chunks,)), dma((chunks,)), dma((chunks,)),
            dma((chunks,)), dma((chunks,)), dma((rows - 1,)), dma((rows - 1,)),
            dma((3,)), dma((chunks,)),
        ],
        compiler_params=pltpu.CompilerParams(
            collective_id=0, has_side_effects=True, vmem_limit_bytes=56 * 1024 * 1024
        ),
    )(activations, up_weight, up_bias.reshape(1, hidden_units), cotangent)

    split = 1
    weight_grad, bias_grad, hidden, act_grad = pl.pallas_call(
        outer_kernel,
        grid=(chunks, split),
        out_shape=(
            jax.ShapeDtypeStruct((feats, hidden_units), BF16),
            jax.ShapeDtypeStruct((1, hidden_units), F32),
            jax.ShapeDtypeStruct((8, hidden_units), BF16),
            jax.ShapeDtypeStruct((8, feats), BF16),
        ),
        in_specs=[
            pl.BlockSpec((32, feats), lambda k, i: (0, 0)),
            pl.BlockSpec((1, 32, width), lambda k, i: (k, 0, 0)),
            any_spec,
            any_spec,
        ],
        out_specs=(
            pl.BlockSpec((feats // split, width), lambda k, i: (i, k)),
            pl.BlockSpec((1, width), lambda k, i: (0, k)),
            any_spec,
            any_spec,
        ),
        scratch_shapes=[pltpu.VMEM((feats, 32), BF16), dma((2,))],
        compiler_params=pltpu.CompilerParams(vmem_limit_bytes=62 * 1024 * 1024),
    )(x_all, grad_all, hidden, act_grad)
    return hidden, act_grad, weight_grad, bias_grad.reshape(hidden_units)


def solution(mesh):
    in_specs = (P(("grp", "row"), "col"), P("col", "row"), P("row"), P(("grp", "col"), "row"))
    out_specs = (
        P(("grp", "col"), "row"),
        P(("grp", "row"), "col"),
        P(("grp", "col"), "row"),
        P(("grp", "row")),
    )
    rows, cols = mesh.shape["row"], mesh.shape["col"]

    def per_device(activations, up_weight, up_bias, cotangent):
        feats, hidden_units = up_weight.shape
        chunks = 8
        fits = (
            rows == 4
            and cols == 4
            and activations.shape[0] == 8
            and cotangent.shape[0] == 8
            and feats % 256 == 0
            and hidden_units % (chunks * 256) == 0
            and feats * hidden_units <= 1536 * 12288
        )
        if fits:
            return fast_per_device(
                activations, up_weight, up_bias, cotangent, rows=rows, chunks=chunks
            )
        return general_per_device(activations, up_weight, up_bias, cotangent)

    return jax.shard_map(
        per_device, mesh=mesh, in_specs=in_specs, out_specs=out_specs, check_vma=False
    )
```
